32 devices in a mesh: ctx: 8 (over z, y), head: 4 (over x, core).
Axes of the slice: x: 2, y: 2, z: 4, core: 2. Of those that a mesh axis runs over, the one named last changes fastest.
Arguments:
- queries: bfloat16 [1024, 2048], P('ctx', 'head'), may hold values from -6 to 6
- keys: bfloat16 [1024, 2048], P('ctx', 'head'), may hold values from -6 to 6
- values: bfloat16 [1024, 4096], P('ctx', 'head'), may hold values from -6 to 6
- out_gate: bfloat16 [1024, 4096], P('ctx', 'head'), may hold values from -6 to 6
- log_decay: float32 [1024, 32], P('ctx', 'head'), may hold values from -1.5 to 0, as said below
- write_strength: float32 [1024, 32], P('ctx', 'head'), may hold values from 0 to 1
- segment_ids: int32 [1024], P('ctx'), may hold values from 0 to 2, never falling along the last dimension, each value on 1 to 512 neighbouring positions
- head_order: int32 [32], replicated, may hold values from 0 to 31, each once
- out_weight: bfloat16 [4096, 2048], P('head'), may hold values from -0.09375 to 0.09375
Outputs:
- layer_out: bfloat16 [1024, 2048], P(('ctx', 'head'))
- decode_states: float32 [32, 16384], P('head', 'ctx')
The draws below stay inside these ranges and needn't reach their ends.
Inputs may be any that keep to these rules, and one draw needn't show every extreme that they name: `log_decay`: Negative.
All inputs are finite; a program needn't handle non-finite values.
Results may differ from the reference program's by a relative error of at most 0.0049.
Values may be sent and summed in bfloat16 or wider, within the bound.
A program may use at most 192 MiB of HBM per device.

```python
import math
import jax
import jax.numpy as jnp
import numpy as np
from jax import lax

D = 2048
HK = 16
VALUE_HEADS = 32
DK = 128
DV = 128
BLOCK = 64
TOK_DEV = 128
WINDOW_TOKENS = 1024
N_CTX = 8


def head_kinds(key):
    kind_key = jax.random.fold_in(key, 7001)
    slow_share = 5
    return jax.random.randint(kind_key, (VALUE_HEADS,), 0, 10) < slow_share


def draw_log_decay(key, part):
    slow_heads = head_kinds(key)
    random_subkeys = jax.random.split(jax.random.fold_in(key, 7002), 6)
    slow_rate = jnp.exp(jax.random.uniform(random_subkeys[0], (VALUE_HEADS,), minval=math.log(0.2), maxval=0.0)) * math.log(10.0) / WINDOW_TOKENS
    fast_rate = 1.0 / jax.random.uniform(random_subkeys[1], (VALUE_HEADS,), minval=30.0, maxval=50.0)
    head_rate = jnp.where(slow_heads, slow_rate, fast_rate)
    block_factor = jnp.exp(jax.random.uniform(random_subkeys[2], (WINDOW_TOKENS // TOK_DEV, VALUE_HEADS), minval=math.log(0.5), maxval=math.log(2.0)))
    block_factor = jnp.repeat(block_factor, TOK_DEV, axis=0)
    token_factor = jnp.exp(jax.random.uniform(random_subkeys[3], (WINDOW_TOKENS, VALUE_HEADS), minval=math.log(0.5), maxval=math.log(2.0)))
    surge_position = jax.random.randint(random_subkeys[4], (3, VALUE_HEADS), 0, WINDOW_TOKENS)
    token_positions = jnp.arange(WINDOW_TOKENS)[:, None, None]
    surge_active = jnp.any(token_positions == surge_position[None, :, :], axis=1)
    surge_falloff = jnp.log(jax.random.uniform(random_subkeys[5], (WINDOW_TOKENS, VALUE_HEADS), minval=0.5, maxval=0.8))
    smoothed_rows = -head_rate[None, :] * block_factor * token_factor
    return (smoothed_rows + jnp.where(surge_active, surge_falloff, 0.0)).astype(jnp.float32)


def draw_write_strength(key, part):
    slow_heads = head_kinds(key)
    random_subkeys = jax.random.split(jax.random.fold_in(key, 7003), 2)
    slow_value = jnp.exp(jax.random.uniform(random_subkeys[0], (WINDOW_TOKENS, VALUE_HEADS), minval=math.log(0.1), maxval=0.0)) * 0.8 * DK / WINDOW_TOKENS
    fast_value = jax.random.uniform(random_subkeys[1], (WINDOW_TOKENS, VALUE_HEADS), minval=0.2, maxval=0.95)
    return jnp.where(slow_heads[None, :], slow_value, fast_value).astype(jnp.float32)


def block_scale(key, extent, cuts, low, top_value):
    gain = 1.0
    for axis_at, blocks in cuts:
        steps = jax.random.uniform(jax.random.fold_in(jax.random.fold_in(key, 6), axis_at), (blocks,), jnp.float32, low / len(cuts), top_value / len(cuts))
        gain = gain * jnp.repeat(jnp.exp(steps), extent[axis_at] // blocks).reshape((-1,) + (1,) * (len(extent) - 1 - axis_at))
    return gain


def profile(amount, total, limit, skew):
    loads = [(1 << 20) // math.isqrt(rank ** skew) + 1 for rank in range(2, amount + 1)]
    rest, holding = total - limit - (amount - 1), [1] * (amount - 1)
    while rest > 0:
        candidates = [i for i in range(amount - 1) if holding[i] < limit]
        mass, remaining = sum([loads[i] for i in candidates]), rest
        for i in candidates:
            more = min(limit - holding[i], max(1, remaining * loads[i] // mass), rest)
            holding[i] = holding[i] + more
            rest = rest - more
    return np.array([limit] + holding)


def uneven(rng, amount, total, reach, slope):
    if amount == 2:
        one = jax.random.randint(rng, (), max(1, total - reach), min(reach, total - 1) + 1)
        return jnp.stack([one, total - one])
    tallies = jnp.asarray(profile(amount, total, reach, slope), jnp.int32)
    couples = (amount - 1) // 2
    source_of, sink = tallies[1:1 + 2 * couples:2], tallies[2:2 + 2 * couples:2]
    margin = jnp.minimum(source_of - 1, reach - sink)
    passed = jax.random.randint(jax.random.fold_in(rng, 1), (couples,), 0, 1 << 20) % (margin + 1)
    tallies = tallies.at[1:1 + 2 * couples:2].set(source_of - passed).at[2:2 + 2 * couples:2].set(sink + passed)
    return tallies[jax.random.permutation(jax.random.fold_in(rng, 2), amount)]


def gaussian(stream_key, shape, deviation, reach, cuts=(), held_as=jnp.bfloat16):
    values = deviation * jax.random.normal(stream_key, shape, jnp.float32)
    if cuts:
        values = values * block_scale(stream_key, shape, cuts, -0.22, 0.18)
    return jnp.clip(values, -reach, reach).astype(held_as)


def setup_inputs(seed: int = 0) -> dict:
    key_of = jax.random.split(jax.random.key(seed), 10)
    queries = gaussian(key_of[0], (WINDOW_TOKENS, HK * DK), 1.0, 6.0, ((0, 8), (1, 4)))
    keys = gaussian(key_of[1], (WINDOW_TOKENS, HK * DK), 1.0, 6.0, ((0, 8), (1, 4)))
    values = gaussian(key_of[2], (WINDOW_TOKENS, VALUE_HEADS * DV), 1.0, 6.0, ((0, 8), (1, 4)))
    out_gate = gaussian(key_of[3], (WINDOW_TOKENS, VALUE_HEADS * DV), 1.0, 6.0, ((0, 8), (1, 4)))
    log_decay = draw_log_decay(jax.random.fold_in(key_of[9], 71), 0)
    write_strength = draw_write_strength(jax.random.fold_in(key_of[9], 71), 0)
    segment_ids = jnp.searchsorted(jnp.cumsum(uneven(key_of[6], max(3, N_CTX // 16), WINDOW_TOKENS, WINDOW_TOKENS // 2, 0)), jnp.arange(WINDOW_TOKENS), side="right").astype(jnp.int32)
    head_order = jax.random.permutation(key_of[7], VALUE_HEADS).astype(jnp.int32)
    out_weight = gaussian(key_of[8], (VALUE_HEADS * DV, D), (VALUE_HEADS * DV) ** -0.5, 0.09375, ((0, 4),))
    return dict(queries=queries, keys=keys, values=values, out_gate=out_gate, log_decay=log_decay, write_strength=write_strength, segment_ids=segment_ids, head_order=head_order, out_weight=out_weight)


highest = lax.Precision.HIGHEST
norm_eps = 1e-06

def product(form, left, right):
    return jnp.einsum(form, left, right, precision=highest)

def unit_rows(raw_rows, scaling):
    widened = raw_rows.astype(jnp.float32)
    return widened * lax.rsqrt(lax.optimization_barrier(jnp.sum(widened * widened, axis=-1, keepdims=True)) + norm_eps) * scaling

def gated_norm(attention, gate_rows):
    mean_square = lax.optimization_barrier(jnp.mean(attention * attention, axis=-1, keepdims=True))
    gated = attention * lax.rsqrt(mean_square + norm_eps) * jax.nn.silu(gate_rows.astype(jnp.float32))
    return gated.astype(jnp.bfloat16)

def inverse_unit_lower(coupling):
    block_size = coupling.shape[-1]
    identity_matrix = jnp.eye(block_size, dtype=jnp.float32)
    inverse = identity_matrix - coupling
    squared = coupling
    for doubling in range(block_size.bit_length() - 2):
        squared = product('...ij,...jk->...ik', squared, squared)
        inverse = product('...ij,...jk->...ik', inverse, identity_matrix + squared)
    return inverse

def block_parts(query_part, key_part, value_part, decay_rows, strength_rows, doc_rows, doc_before):
    block_size = doc_rows.shape[-1]
    token_positions = jnp.arange(block_size)
    causal = token_positions[:, None] >= token_positions[None, :]
    strict = token_positions[:, None] > token_positions[None, :]
    same_doc = (doc_rows[..., :, None] == doc_rows[..., None, :]) & causal
    continues = doc_rows == doc_before[..., None]
    cumulative = jnp.cumsum(decay_rows, axis=-1)
    decay_gap = cumulative[..., :, None] - cumulative[..., None, :]
    mixing = jnp.where(same_doc[..., None, :, :], jnp.exp(jnp.minimum(decay_gap, 0.0)), 0.0)
    entry_decay = jnp.where(continues[..., None, :], jnp.exp(cumulative), 0.0)
    key_intersection = product('...id,...jd->...ij', key_part, key_part)
    coupling = jnp.where(strict, strength_rows[..., :, None] * mixing * key_intersection, 0.0)
    inverse = inverse_unit_lower(coupling)
    weighted = product('...ij,...jd->...id', inverse, (strength_rows * entry_decay)[..., None] * key_part)
    pseudo_values = product('...ij,...jd->...id', inverse, strength_rows[..., None] * value_part)
    masked_scores = mixing * product('...id,...jd->...ij', query_part, key_part)
    local_out = product('...ij,...jd->...id', masked_scores, pseudo_values)
    state_read = entry_decay[..., None] * query_part - product('...ij,...jd->...id', masked_scores, weighted)
    last_keys = mixing[..., -1, :, None] * key_part
    identity_map = jnp.eye(key_part.shape[-1], dtype=jnp.float32)
    transition = entry_decay[..., -1, None, None] * identity_map - product('...jd,...je->...de', last_keys, weighted)
    written = product('...jd,...je->...de', last_keys, pseudo_values)
    return (local_out, state_read, transition, written)

def reference(queries, keys, values, out_gate, log_decay, write_strength, segment_ids, head_order, out_weight):
    tokens = queries.shape[0]
    blocks = tokens // BLOCK
    group_size = VALUE_HEADS // HK
    doc_blocks = segment_ids.reshape(blocks, BLOCK)
    doc_before = jnp.concatenate([doc_blocks[:1, 0], doc_blocks[:-1, -1]]).astype(jnp.int32)

    def advance(carried, pieces):
        query_raw, key_raw, value_raw, gate_raw, decay_raw, strength_raw, doc_rows, doc_prior = pieces
        query_part = jnp.repeat(unit_rows(query_raw.reshape(BLOCK, HK, DK), DK ** (-0.5)), group_size, axis=1).transpose(1, 0, 2)
        key_part = jnp.repeat(unit_rows(key_raw.reshape(BLOCK, HK, DK), 1.0), group_size, axis=1).transpose(1, 0, 2)
        value_part = value_raw.reshape(BLOCK, VALUE_HEADS, DV).astype(jnp.float32).transpose(1, 0, 2)
        local_out, state_read, transition, written = block_parts(query_part, key_part, value_part, decay_raw.T, strength_raw.T, doc_rows, doc_prior)
        attention = local_out + product('hid,hde->hie', state_read, carried)
        normed = gated_norm(attention.transpose(1, 0, 2), gate_raw.reshape(BLOCK, VALUE_HEADS, DV)).reshape(BLOCK, VALUE_HEADS * DV)
        projected = jnp.dot(normed, out_weight, preferred_element_type=jnp.float32).astype(jnp.bfloat16)
        return (product('hde,hef->hdf', transition, carried) + written, projected)
    inputs = (queries.reshape(blocks, BLOCK, HK * DK), keys.reshape(blocks, BLOCK, HK * DK), values.reshape(blocks, BLOCK, VALUE_HEADS * DV), out_gate.reshape(blocks, BLOCK, VALUE_HEADS * DV), log_decay.reshape(blocks, BLOCK, VALUE_HEADS), write_strength.reshape(blocks, BLOCK, VALUE_HEADS), doc_blocks, doc_before)
    final_state, outputs = lax.scan(advance, jnp.zeros((VALUE_HEADS, DK, DV), jnp.float32), inputs)
    decode_states = jnp.take(final_state.reshape(VALUE_HEADS, DK * DV), head_order, axis=0)
    return (outputs.reshape(tokens, D), decode_states)
```

```python
import functools

import jax
import jax.numpy as jnp
from jax import lax
from jax.experimental import pallas as pl
from jax.experimental.pallas import tpu as pltpu
from jax.sharding import PartitionSpec as P

DK = 128
DV = 128
BLOCK = 64


highest = lax.Precision.HIGHEST
norm_eps = 1e-06


def prefix(x, axis, combine, identity):
    peers, index = (lax.axis_size(axis), lax.axis_index(axis))
    everything = jax.tree.map(lambda part: lax.all_gather(part, axis), x)
    start = jax.tree.map(
        lambda part, zero: jnp.broadcast_to(jnp.asarray(zero, part.dtype), part.shape), x, identity
    )

    def step(k, before):
        reached = k < index
        new = combine(before, jax.tree.map(lambda part: part[k], everything))
        return jax.tree.map(lambda a, b: jnp.where(reached, a, b), new, before)

    return lax.fori_loop(0, peers, step, start)


def product(form, left, right):
    return jnp.einsum(form, left, right, precision=highest)


def unit_rows(raw_rows, scaling):
    widened = raw_rows.astype(jnp.float32)
    return (
        widened * lax.rsqrt(jnp.sum(widened * widened, axis=-1, keepdims=True) + norm_eps) * scaling
    )


def gated_norm(attention, gate_rows):
    mean_square = jnp.mean(attention * attention, axis=-1, keepdims=True)
    gated = (
        attention * lax.rsqrt(mean_square + norm_eps) * jax.nn.silu(gate_rows.astype(jnp.float32))
    )
    return gated.astype(jnp.bfloat16)


def inverse_unit_lower(coupling):
    block_size = coupling.shape[-1]
    identity_matrix = jnp.eye(block_size, dtype=jnp.float32)
    inverse = identity_matrix - coupling
    squared = coupling
    for doubling in range(block_size.bit_length() - 2):
        squared = product("...ij,...jk->...ik", squared, squared)
        inverse = product("...ij,...jk->...ik", inverse, identity_matrix + squared)
    return inverse


def block_parts(query_part, key_part, value_part, decay_rows, strength_rows, doc_rows, doc_before):
    block_size = doc_rows.shape[-1]
    token_positions = jnp.arange(block_size)
    causal = token_positions[:, None] >= token_positions[None, :]
    strict = token_positions[:, None] > token_positions[None, :]
    same_doc = (doc_rows[..., :, None] == doc_rows[..., None, :]) & causal
    continues = doc_rows == doc_before[..., None]
    cumulative = jnp.cumsum(decay_rows, axis=-1)
    decay_gap = cumulative[..., :, None] - cumulative[..., None, :]
    mixing = jnp.where(same_doc[..., None, :, :], jnp.exp(jnp.minimum(decay_gap, 0.0)), 0.0)
    entry_decay = jnp.where(continues[..., None, :], jnp.exp(cumulative), 0.0)
    key_intersection = product("...id,...jd->...ij", key_part, key_part)
    coupling = jnp.where(strict, strength_rows[..., :, None] * mixing * key_intersection, 0.0)
    inverse = inverse_unit_lower(coupling)
    weighted = product(
        "...ij,...jd->...id", inverse, (strength_rows * entry_decay)[..., None] * key_part
    )
    pseudo_values = product("...ij,...jd->...id", inverse, strength_rows[..., None] * value_part)
    masked_scores = mixing * product("...id,...jd->...ij", query_part, key_part)
    local_out = product("...ij,...jd->...id", masked_scores, pseudo_values)
    state_read = entry_decay[..., None] * query_part - product(
        "...ij,...jd->...id", masked_scores, weighted
    )
    last_keys = mixing[..., -1, :, None] * key_part
    identity_map = jnp.eye(key_part.shape[-1], dtype=jnp.float32)
    transition = entry_decay[..., -1, None, None] * identity_map - product(
        "...jd,...je->...de", last_keys, weighted
    )
    written = product("...jd,...je->...de", last_keys, pseudo_values)
    return (local_out, state_read, transition, written)


def combine_spans(earlier, later):
    linked = jnp.where((earlier[3] < 0) | (later[2] < 0) | (earlier[3] == later[2]), 1.0, 0.0)
    through = linked * product("hde,hef->hdf", later[0], earlier[0])
    reached = linked * product("hde,hef->hdf", later[0], earlier[1]) + later[1]
    first_doc = jnp.where(earlier[2] >= 0, earlier[2], later[2])
    last_doc = jnp.where(later[3] >= 0, later[3], earlier[3])
    return (through, reached, first_doc, last_doc)


def gathered_prefix(
    queries, keys, values, out_gate, log_decay, write_strength, segment_ids, head_order, out_weight
):
    tok_rows = queries.shape[0]
    heads_here = values.shape[1] // DV
    key_groups = queries.shape[1] // DK
    group_size = heads_here // key_groups
    blocks = tok_rows // BLOCK

    def head_major(raw_rows, scaling):
        unit_part = unit_rows(raw_rows.reshape(blocks, BLOCK, key_groups, DK), scaling)
        return jnp.repeat(unit_part, group_size, axis=2).transpose(0, 2, 1, 3)

    query_part = head_major(queries, DK ** (-0.5))
    key_part = head_major(keys, 1.0)
    value_part = (
        values.reshape(blocks, BLOCK, heads_here, DV).astype(jnp.float32).transpose(0, 2, 1, 3)
    )
    decay_rows = log_decay.reshape(blocks, BLOCK, heads_here).transpose(0, 2, 1)
    strength_rows = write_strength.reshape(blocks, BLOCK, heads_here).transpose(0, 2, 1)
    doc_blocks = segment_ids.reshape(blocks, BLOCK)
    doc_before = jnp.concatenate([doc_blocks[:1, 0], doc_blocks[:-1, -1]])
    local_out, state_read, transition, written = block_parts(
        query_part, key_part, value_part, decay_rows, strength_rows, doc_blocks, doc_before
    )
    identity_map = jnp.broadcast_to(jnp.eye(DK, dtype=jnp.float32), (heads_here, DK, DK))
    zero_state = jnp.zeros((heads_here, DK, DV), jnp.float32)

    def compose_keep(carried, pieces):
        through, reached = carried
        step_map, step_add = pieces
        updated = (
            product("hde,hef->hdf", step_map, through),
            product("hde,hef->hdf", step_map, reached) + step_add,
        )
        return (updated, carried)

    (whole_map, whole_add), (prefix_maps, prefix_states) = lax.scan(
        compose_keep, (identity_map, zero_state), (transition, written)
    )
    early_out = local_out + product("chid,chde->chie", state_read, prefix_states)
    first_doc = doc_blocks[0, 0].astype(jnp.float32)
    last_doc = doc_blocks[-1, -1].astype(jnp.float32)
    identity = (identity_map, zero_state, jnp.float32(-1.0), jnp.float32(-1.0))
    before = prefix((whole_map, whole_add, first_doc, last_doc), "ctx", combine_spans, identity)
    linked = jnp.where((before[3] < 0) | (before[3] == first_doc), 1.0, 0.0)
    incoming = linked * before[1]
    reach = product("chde,hef->chdf", prefix_maps, incoming)
    attention = early_out + product("chid,chde->chie", state_read, reach)
    final_state = product("hde,hef->hdf", whole_map, incoming) + whole_add
    tokens_major = attention.transpose(0, 2, 1, 3).reshape(tok_rows, heads_here, DV)
    normed = gated_norm(tokens_major, out_gate.reshape(tok_rows, heads_here, DV)).reshape(
        tok_rows, heads_here * DV
    )
    summed = lax.psum_scatter(
        jnp.dot(normed, out_weight, preferred_element_type=jnp.float32),
        "head",
        scatter_dimension=0,
        tiled=True,
    )
    layer_out = summed.astype(jnp.bfloat16)
    groups = lax.axis_size("ctx")
    is_last = jnp.where(lax.axis_index("ctx") == groups - 1, 1.0, 0.0).astype(jnp.float32)
    own_columns = lax.psum_scatter(
        final_state.reshape(heads_here, DK * DV) * is_last, "ctx", scatter_dimension=1, tiled=True
    )
    every_head = lax.all_gather(own_columns, "head", axis=0, tiled=True)
    order_here = lax.dynamic_slice_in_dim(
        head_order, lax.axis_index("head") * heads_here, heads_here, 0
    )
    selector = (
        order_here[:, None] == jnp.arange(every_head.shape[0], dtype=jnp.int32)[None, :]
    ).astype(jnp.float32)
    decode_states = product("jh,hw->jw", selector, every_head)
    return (layer_out, decode_states)


MESH = pl.DeviceIdType.MESH
COLUMN_TILE = 512
META_ROWS = 16


def mxu(left, right):
    return jnp.dot(
        left.astype(jnp.bfloat16), right.astype(jnp.bfloat16), preferred_element_type=jnp.float32
    )


def inverse_by_halves(coupling, row_at, col_at):
    size = coupling.shape[0]
    eye = (row_at == col_at).astype(jnp.float32)
    inverse = eye - jnp.where(row_at // 2 == col_at // 2, coupling, 0.0)
    half = 2
    while half < size:
        within = (row_at // (2 * half) == col_at // (2 * half)) & (row_at // half != col_at // half)
        below = jnp.where(within, coupling, 0.0)
        inverse = inverse - mxu(mxu(inverse, below), inverse)
        half *= 2
    return inverse


def layer_kernel(
    ctx_size,
    head_size,
    q_ref,
    k_ref,
    v_ref,
    gate_ref,
    decay_ref,
    strength_ref,
    doc_ref,
    order_ref,
    weight_ref,
    out_ref,
    decode_ref,
    weight,
    decay_cols,
    strength_cols,
    decay_rows,
    outbox,
    inbox,
    entering,
    arrived,
    local,
    reader,
    normed,
    final,
    columns,
    partial,
    leaving,
    summands,
    weight_sem,
    map_send,
    map_recv,
    state_send,
    state_recv,
    final_send,
    final_recv,
    column_send,
    column_recv,
    sum_send,
    sum_recv,
):
    me = lax.axis_index("ctx")
    group = lax.axis_index("head")
    rows = q_ref.shape[0]
    key_groups = q_ref.shape[1] // DK
    heads = v_ref.shape[1] // DV
    share = heads // key_groups
    own_rows = rows // head_size
    state_rows = DK // ctx_size
    width = weight.shape[1]
    tiles = width // COLUMN_TILE

    barrier = pltpu.get_barrier_semaphore()
    for away in range(1, ctx_size):
        pl.semaphore_signal(
            barrier, inc=1, device_id=(lax.rem(me + away, ctx_size), group), device_id_type=MESH
        )
    for away in range(1, head_size):
        pl.semaphore_signal(
            barrier, inc=1, device_id=(me, lax.rem(group + away, head_size)), device_id_type=MESH
        )
    fetch = pltpu.make_async_copy(weight_ref, weight, weight_sem)
    fetch.start()

    row_at = lax.broadcasted_iota(jnp.int32, (rows, rows), 0)
    col_at = lax.broadcasted_iota(jnp.int32, (rows, rows), 1)
    causal = row_at >= col_at
    strict = row_at > col_at
    eye = (row_at == col_at).astype(jnp.float32)
    cumulative = jnp.dot(
        causal.astype(jnp.float32),
        decay_ref[...],
        precision=highest,
        preferred_element_type=jnp.float32,
    )
    for h in range(heads):
        spread = jnp.broadcast_to(cumulative[:, h : h + 1], (rows, rows))
        decay_cols[h] = spread
        decay_rows[h] = spread.T[0:8]
        strength_cols[h] = jnp.broadcast_to(strength_ref[:, h : h + 1], (rows, rows))
    doc_row = doc_ref[...].astype(jnp.float32)
    doc_cols = jnp.broadcast_to(doc_row, (rows, rows)).T
    same_doc = (doc_cols == doc_row) & causal
    first_doc = doc_cols[0:1]
    last_doc = doc_cols[rows - 1 : rows]
    continues = doc_cols == first_doc
    meta_at = lax.broadcasted_iota(jnp.int32, (META_ROWS, rows), 0)

    pl.semaphore_wait(barrier, ctx_size - 1 + head_size - 1)

    def map_copy(h):
        return pltpu.make_async_remote_copy(
            src_ref=outbox.at[h],
            dst_ref=inbox.at[me],
            send_sem=map_send.at[h],
            recv_sem=map_recv.at[me],
            device_id=(h, group),
            device_id_type=MESH,
        )

    def key_group(turn, _):
        kh = lax.rem(me // share + 1 + turn, key_groups)
        at = pl.ds(pl.multiple_of(kh * DK, DK), DK)
        query_raw = q_ref[:, at]
        key_raw = k_ref[:, at]
        query_wide = query_raw.astype(jnp.float32)
        key_wide = key_raw.astype(jnp.float32)
        query_scale = lax.rsqrt(
            jnp.sum(query_wide * query_wide, axis=-1, keepdims=True) + norm_eps
        ) * DK ** (-0.5)
        key_scale = lax.rsqrt(jnp.sum(key_wide * key_wide, axis=-1, keepdims=True) + norm_eps)
        query_part = query_wide * query_scale
        key_part = key_wide * key_scale
        key_across = key_part.T
        key_scale_row = jnp.broadcast_to(key_scale, (rows, rows)).T
        raw_across = key_wide.T
        key_overlap = mxu(key_raw, raw_across) * key_scale * key_scale_row
        query_overlap = mxu(query_raw, raw_across) * query_scale * key_scale_row
        for member in range(share):
            h = kh * share + member
            decay = decay_cols[h]
            strength = strength_cols[h]
            mixing = jnp.where(
                same_doc, jnp.exp(jnp.minimum(decay - decay_rows[h][0:1], 0.0)), 0.0
            )
            entry = jnp.where(continues, jnp.exp(decay), 0.0)
            coupling = jnp.where(strict, strength * mixing * key_overlap, 0.0)
            inverse = inverse_by_halves(coupling, row_at, col_at)
            value_at = pl.ds(pl.multiple_of(h * DV, DV), DV)
            value_part = v_ref[:, value_at].astype(jnp.float32)
            sides = jnp.concatenate(
                [strength * entry * key_part, strength * value_part], axis=1
            )
            sides = sides + mxu(inverse - eye, sides)
            seen = mxu(mixing * query_overlap, sides)
            local[h] = seen[:, DK:]
            reader[h] = (entry * query_part - seen[:, :DK]).astype(jnp.bfloat16)
            moved = mxu(key_across * mixing[rows - 1 : rows], sides)
            outbox[h, 0:DK, :] = (-moved[:, :DK]).astype(jnp.bfloat16)
            outbox[h, DK : 2 * DK, :] = moved[:, DK:].astype(jnp.bfloat16)
            kept = entry[rows - 1 : rows]
            kept_high = kept.astype(jnp.bfloat16).astype(jnp.float32)
            meta = jnp.where(
                meta_at == 0,
                kept_high,
                jnp.where(
                    meta_at == 1, kept - kept_high, jnp.where(meta_at == 2, first_doc, last_doc)
                ),
            )
            outbox[h, 2 * DK : 2 * DK + META_ROWS, :] = meta.astype(jnp.bfloat16)
        for member in range(share):
            h = kh * share + member

            @pl.when(h != me)
            def _():
                map_copy(h).start()

            @pl.when(h == me)
            def _():
                inbox[me] = outbox[me]

        return 0

    lax.fori_loop(0, key_groups, key_group, 0)

    def state_copy(i):
        return pltpu.make_async_remote_copy(
            src_ref=entering.at[i],
            dst_ref=arrived.at[me],
            send_sem=state_send.at[i],
            recv_sem=state_recv.at[me],
            device_id=(i, group),
            device_id_type=MESH,
        )

    def landed(buffer, slot, send, recv):
        return pltpu.make_async_remote_copy(
            src_ref=buffer.at[slot],
            dst_ref=buffer.at[slot],
            send_sem=send.at[slot],
            recv_sem=recv.at[slot],
            device_id=(slot, group),
            device_id_type=MESH,
        )

    state = jnp.zeros((DK, DV), jnp.float32)
    doc_before = None
    for i in range(ctx_size):

        @pl.when(me != i)
        def _():
            landed(inbox, i, map_send, map_recv).wait_recv()

        meta = inbox[i, 2 * DK : 2 * DK + META_ROWS, :].astype(jnp.float32)
        if i > 0:
            state = jnp.where(meta[2:3] == doc_before, state, 0.0)
        doc_before = meta[3:4]
        state_low = state.astype(jnp.bfloat16)
        entering[i] = state_low

        @pl.when(me != i)
        def _():
            state_copy(i).start()

        @pl.when(me == i)
        def _():
            arrived[i] = entering[i]

        added = inbox[i, DK : 2 * DK, :].astype(jnp.float32)
        state = (meta[0:1] + meta[1:2]) * state + mxu(inbox[i, 0:DK, :], state_low) + added
    final[...] = state

    head_here = group * heads + me

    def final_copy(c):
        return pltpu.make_async_remote_copy(
            src_ref=final.at[pl.ds(pl.multiple_of(c * state_rows, state_rows), state_rows)],
            dst_ref=columns.at[head_here],
            send_sem=final_send.at[c],
            recv_sem=final_recv.at[me],
            device_id=(c, group),
            device_id_type=MESH,
        )

    for away in range(1, ctx_size):
        final_copy(lax.rem(me + away, ctx_size)).start()
    columns[head_here] = final[pl.ds(pl.multiple_of(me * state_rows, state_rows), state_rows)]

    for h in range(heads):

        @pl.when(me != h)
        def _():
            landed(arrived, h, state_send, state_recv).wait_recv()

        attention = local[h] + mxu(reader[h], arrived[h])
        mean_square = jnp.mean(attention * attention, axis=-1, keepdims=True)
        gate = gate_ref[:, h * DV : (h + 1) * DV].astype(jnp.float32)
        gated = attention * lax.rsqrt(mean_square + norm_eps) * (gate / (1.0 + jnp.exp(-gate)))
        normed[:, h * DV : (h + 1) * DV] = gated.astype(jnp.bfloat16)

    fetch.wait()

    def sum_copy(tile, away):
        peer = lax.rem(group + away, head_size)
        return pltpu.make_async_remote_copy(
            src_ref=leaving.at[tile, pl.ds(pl.multiple_of(peer * own_rows, own_rows), own_rows)],
            dst_ref=summands.at[tile, away],
            send_sem=sum_send.at[tile, away],
            recv_sem=sum_recv.at[tile, away],
            device_id=(me, peer),
            device_id_type=MESH,
        )

    for tile in range(tiles):
        at = slice(tile * COLUMN_TILE, (tile + 1) * COLUMN_TILE)
        product_here = jnp.dot(normed[...], weight[:, at], preferred_element_type=jnp.float32)
        partial[:, at] = product_here
        leaving[tile] = product_here.astype(jnp.bfloat16)
        for away in range(1, head_size):
            sum_copy(tile, away).start()

    for away in range(1, ctx_size):
        source = lax.rem(me + away, ctx_size)
        pltpu.make_async_remote_copy(
            src_ref=columns.at[group * heads + source],
            dst_ref=columns.at[group * heads + source],
            send_sem=final_send.at[source],
            recv_sem=final_recv.at[source],
            device_id=(source, group),
            device_id_type=MESH,
        ).wait_recv()

    def column_copy(peer, block, slot):
        return pltpu.make_async_remote_copy(
            src_ref=columns.at[pl.ds(block * heads, heads)],
            dst_ref=columns.at[pl.ds(block * heads, heads)],
            send_sem=column_send.at[slot],
            recv_sem=column_recv.at[slot],
            device_id=(me, peer),
            device_id_type=MESH,
        )

    for away in range(1, head_size):
        column_copy(lax.rem(group + away, head_size), group, away).start()

    for tile in range(tiles):
        at = slice(tile * COLUMN_TILE, (tile + 1) * COLUMN_TILE)
        total = partial[pl.ds(pl.multiple_of(group * own_rows, own_rows), own_rows), at]
        for away in range(1, head_size):
            sum_copy(tile, away).wait_recv()
            total = total + summands[tile, away].astype(jnp.float32)
        out_ref[:, at] = total.astype(jnp.bfloat16)

    for away in range(1, head_size):
        source = lax.rem(group + head_size - away, head_size)
        column_copy(source, source, away).wait_recv()
    for slot in range(heads):
        chosen = columns[order_ref[group * heads + slot]]
        for r in range(state_rows):
            decode_ref[slot : slot + 1, r * DV : (r + 1) * DV] = chosen[r : r + 1]

    for away in range(1, ctx_size):
        other = lax.rem(me + away, ctx_size)
        map_copy(other).wait_send()
        state_copy(other).wait_send()
        final_copy(other).wait_send()
    for away in range(1, head_size):
        column_copy(lax.rem(group + away, head_size), group, away).wait_send()
        for tile in range(tiles):
            sum_copy(tile, away).wait_send()


def head_owner(
    queries, keys, values, out_gate, log_decay, write_strength, segment_ids, head_order, out_weight
):
    rows = queries.shape[0]
    heads = values.shape[1] // DV
    ctx_size, head_size = lax.axis_size("ctx"), lax.axis_size("head")
    width = out_weight.shape[1]
    tiles = width // COLUMN_TILE
    own_rows = rows // head_size
    state_rows = DK // ctx_size
    f32, bf16 = jnp.float32, jnp.bfloat16
    dma = pltpu.SemaphoreType.DMA
    vmem = pl.BlockSpec(memory_space=pltpu.VMEM)
    return pl.pallas_call(
        functools.partial(layer_kernel, ctx_size, head_size),
        out_shape=(
            jax.ShapeDtypeStruct((own_rows, width), bf16),
            jax.ShapeDtypeStruct((heads, state_rows * DV), f32),
        ),
        in_specs=[vmem] * 7
        + [pl.BlockSpec(memory_space=pltpu.SMEM), pl.BlockSpec(memory_space=pl.ANY)],
        out_specs=(vmem, vmem),
        scratch_shapes=[
            pltpu.VMEM(out_weight.shape, bf16),
            pltpu.VMEM((heads, rows, rows), f32),
            pltpu.VMEM((heads, rows, rows), f32),
            pltpu.VMEM((heads, 8, rows), f32),
            pltpu.VMEM((heads, 2 * DK + META_ROWS, DV), bf16),
            pltpu.VMEM((ctx_size, 2 * DK + META_ROWS, DV), bf16),
            pltpu.VMEM((ctx_size, DK, DV), bf16),
            pltpu.VMEM((heads, DK, DV), bf16),
            pltpu.VMEM((heads, rows, DV), f32),
            pltpu.VMEM((heads, rows, DK), bf16),
            pltpu.VMEM((rows, heads * DV), bf16),
            pltpu.VMEM((DK, DV), f32),
            pltpu.VMEM((head_size * heads, state_rows, DV), f32),
            pltpu.VMEM((rows, width), f32),
            pltpu.VMEM((tiles, rows, COLUMN_TILE), bf16),
            pltpu.VMEM((tiles, head_size, own_rows, COLUMN_TILE), bf16),
            dma,
            dma((heads,)),
            dma((ctx_size,)),
            dma((ctx_size,)),
            dma((heads,)),
            dma((ctx_size,)),
            dma((ctx_size,)),
            dma((head_size,)),
            dma((head_size,)),
            dma((tiles, head_size)),
            dma((tiles, head_size)),
        ],
        compiler_params=pltpu.CompilerParams(
            collective_id=0, has_side_effects=True, vmem_limit_bytes=40 * 1024 * 1024
        ),
    )(
        queries,
        keys,
        values,
        out_gate,
        log_decay,
        write_strength,
        segment_ids.reshape(1, rows),
        head_order,
        out_weight,
    )


def per_device(queries, keys, values, *rest):
    heads = values.shape[1] // DV
    one_owner_per_head = heads == lax.axis_size("ctx") and queries.shape[0] == DK
    form = head_owner if one_owner_per_head else gathered_prefix
    return form(queries, keys, values, *rest)


def solution(mesh):
    in_specs = (
        P("ctx", "head"),
        P("ctx", "head"),
        P("ctx", "head"),
        P("ctx", "head"),
        P("ctx", "head"),
        P("ctx", "head"),
        P("ctx"),
        P(),
        P("head", None),
    )
    out_specs = (P(("ctx", "head"), None), P("head", "ctx"))
    return jax.shard_map(
        per_device, mesh=mesh, in_specs=in_specs, out_specs=out_specs, check_vma=False
    )
```

```python
import functools

import jax
import jax.numpy as jnp
from jax import lax
from jax.experimental import pallas as pl
from jax.experimental.pallas import tpu as pltpu
from jax.sharding import PartitionSpec as P

DK = 128
DV = 128
BLOCK = 64


highest = lax.Precision.HIGHEST
norm_eps = 1e-06


def prefix(x, axis, combine, identity):
    peers, index = (lax.axis_size(axis), lax.axis_index(axis))
    everything = jax.tree.map(lambda part: lax.all_gather(part, axis), x)
    start = jax.tree.map(
        lambda part, zero: jnp.broadcast_to(jnp.asarray(zero, part.dtype), part.shape), x, identity
    )

    def step(k, before):
        reached = k < index
        new = combine(before, jax.tree.map(lambda part: part[k], everything))
        return jax.tree.map(lambda a, b: jnp.where(reached, a, b), new, before)

    return lax.fori_loop(0, peers, step, start)


def product(form, left, right):
    return jnp.einsum(form, left, right, precision=highest)


def unit_rows(raw_rows, scaling):
    widened = raw_rows.astype(jnp.float32)
    return (
        widened * lax.rsqrt(jnp.sum(widened * widened, axis=-1, keepdims=True) + norm_eps) * scaling
    )


def gated_norm(attention, gate_rows):
    mean_square = jnp.mean(attention * attention, axis=-1, keepdims=True)
    gated = (
        attention * lax.rsqrt(mean_square + norm_eps) * jax.nn.silu(gate_rows.astype(jnp.float32))
    )
    return gated.astype(jnp.bfloat16)


def inverse_unit_lower(coupling):
    block_size = coupling.shape[-1]
    identity_matrix = jnp.eye(block_size, dtype=jnp.float32)
    inverse = identity_matrix - coupling
    squared = coupling
    for doubling in range(block_size.bit_length() - 2):
        squared = product("...ij,...jk->...ik", squared, squared)
        inverse = product("...ij,...jk->...ik", inverse, identity_matrix + squared)
    return inverse


def block_parts(query_part, key_part, value_part, decay_rows, strength_rows, doc_rows, doc_before):
    block_size = doc_rows.shape[-1]
    token_positions = jnp.arange(block_size)
    causal = token_positions[:, None] >= token_positions[None, :]
    strict = token_positions[:, None] > token_positions[None, :]
    same_doc = (doc_rows[..., :, None] == doc_rows[..., None, :]) & causal
    continues = doc_rows == doc_before[..., None]
    cumulative = jnp.cumsum(decay_rows, axis=-1)
    decay_gap = cumulative[..., :, None] - cumulative[..., None, :]
    mixing = jnp.where(same_doc[..., None, :, :], jnp.exp(jnp.minimum(decay_gap, 0.0)), 0.0)
    entry_decay = jnp.where(continues[..., None, :], jnp.exp(cumulative), 0.0)
    key_intersection = product("...id,...jd->...ij", key_part, key_part)
    coupling = jnp.where(strict, strength_rows[..., :, None] * mixing * key_intersection, 0.0)
    inverse = inverse_unit_lower(coupling)
    weighted = product(
        "...ij,...jd->...id", inverse, (strength_rows * entry_decay)[..., None] * key_part
    )
    pseudo_values = product("...ij,...jd->...id", inverse, strength_rows[..., None] * value_part)
    masked_scores = mixing * product("...id,...jd->...ij", query_part, key_part)
    local_out = product("...ij,...jd->...id", masked_scores, pseudo_values)
    state_read = entry_decay[..., None] * query_part - product(
        "...ij,...jd->...id", masked_scores, weighted
    )
    last_keys = mixing[..., -1, :, None] * key_part
    identity_map = jnp.eye(key_part.shape[-1], dtype=jnp.float32)
    transition = entry_decay[..., -1, None, None] * identity_map - product(
        "...jd,...je->...de", last_keys, weighted
    )
    written = product("...jd,...je->...de", last_keys, pseudo_values)
    return (local_out, state_read, transition, written)


def combine_spans(earlier, later):
    linked = jnp.where((earlier[3] < 0) | (later[2] < 0) | (earlier[3] == later[2]), 1.0, 0.0)
    through = linked * product("hde,hef->hdf", later[0], earlier[0])
    reached = linked * product("hde,hef->hdf", later[0], earlier[1]) + later[1]
    first_doc = jnp.where(earlier[2] >= 0, earlier[2], later[2])
    last_doc = jnp.where(later[3] >= 0, later[3], earlier[3])
    return (through, reached, first_doc, last_doc)


def gathered_prefix(
    queries, keys, values, out_gate, log_decay, write_strength, segment_ids, head_order, out_weight
):
    tok_rows = queries.shape[0]
    heads_here = values.shape[1] // DV
    key_groups = queries.shape[1] // DK
    group_size = heads_here // key_groups
    blocks = tok_rows // BLOCK

    def head_major(raw_rows, scaling):
        unit_part = unit_rows(raw_rows.reshape(blocks, BLOCK, key_groups, DK), scaling)
        return jnp.repeat(unit_part, group_size, axis=2).transpose(0, 2, 1, 3)

    query_part = head_major(queries, DK ** (-0.5))
    key_part = head_major(keys, 1.0)
    value_part = (
        values.reshape(blocks, BLOCK, heads_here, DV).astype(jnp.float32).transpose(0, 2, 1, 3)
    )
    decay_rows = log_decay.reshape(blocks, BLOCK, heads_here).transpose(0, 2, 1)
    strength_rows = write_strength.reshape(blocks, BLOCK, heads_here).transpose(0, 2, 1)
    doc_blocks = segment_ids.reshape(blocks, BLOCK)
    doc_before = jnp.concatenate([doc_blocks[:1, 0], doc_blocks[:-1, -1]])
    local_out, state_read, transition, written = block_parts(
        query_part, key_part, value_part, decay_rows, strength_rows, doc_blocks, doc_before
    )
    identity_map = jnp.broadcast_to(jnp.eye(DK, dtype=jnp.float32), (heads_here, DK, DK))
    zero_state = jnp.zeros((heads_here, DK, DV), jnp.float32)

    def compose_keep(carried, pieces):
        through, reached = carried
        step_map, step_add = pieces
        updated = (
            product("hde,hef->hdf", step_map, through),
            product("hde,hef->hdf", step_map, reached) + step_add,
        )
        return (updated, carried)

    (whole_map, whole_add), (prefix_maps, prefix_states) = lax.scan(
        compose_keep, (identity_map, zero_state), (transition, written)
    )
    early_out = local_out + product("chid,chde->chie", state_read, prefix_states)
    first_doc = doc_blocks[0, 0].astype(jnp.float32)
    last_doc = doc_blocks[-1, -1].astype(jnp.float32)
    identity = (identity_map, zero_state, jnp.float32(-1.0), jnp.float32(-1.0))
    before = prefix((whole_map, whole_add, first_doc, last_doc), "ctx", combine_spans, identity)
    linked = jnp.where((before[3] < 0) | (before[3] == first_doc), 1.0, 0.0)
    incoming = linked * before[1]
    reach = product("chde,hef->chdf", prefix_maps, incoming)
    attention = early_out + product("chid,chde->chie", state_read, reach)
    final_state = product("hde,hef->hdf", whole_map, incoming) + whole_add
    tokens_major = attention.transpose(0, 2, 1, 3).reshape(tok_rows, heads_here, DV)
    normed = gated_norm(tokens_major, out_gate.reshape(tok_rows, heads_here, DV)).reshape(
        tok_rows, heads_here * DV
    )
    summed = lax.psum_scatter(
        jnp.dot(normed, out_weight, preferred_element_type=jnp.float32),
        "head",
        scatter_dimension=0,
        tiled=True,
    )
    layer_out = summed.astype(jnp.bfloat16)
    groups = lax.axis_size("ctx")
    is_last = jnp.where(lax.axis_index("ctx") == groups - 1, 1.0, 0.0).astype(jnp.float32)
    own_columns = lax.psum_scatter(
        final_state.reshape(heads_here, DK * DV) * is_last, "ctx", scatter_dimension=1, tiled=True
    )
    every_head = lax.all_gather(own_columns, "head", axis=0, tiled=True)
    order_here = lax.dynamic_slice_in_dim(
        head_order, lax.axis_index("head") * heads_here, heads_here, 0
    )
    selector = (
        order_here[:, None] == jnp.arange(every_head.shape[0], dtype=jnp.int32)[None, :]
    ).astype(jnp.float32)
    decode_states = product("jh,hw->jw", selector, every_head)
    return (layer_out, decode_states)


MESH = pl.DeviceIdType.MESH
COLUMN_TILE = 512
META_ROWS = 16


def mxu(left, right):
    return jnp.dot(
        left.astype(jnp.bfloat16), right.astype(jnp.bfloat16), preferred_element_type=jnp.float32
    )


def split(wide):
    high = wide.astype(jnp.bfloat16)
    return high, (wide - high.astype(jnp.float32)).astype(jnp.bfloat16)


def mxu_wide_left(left, right):
    high, low = split(left)
    right = right.astype(jnp.bfloat16)
    return mxu(jnp.concatenate([high, low], axis=1), jnp.concatenate([right, right], axis=0))


def mxu_wide(left, right):
    left_high, left_low = split(left)
    right_high, right_low = split(right)
    return mxu(
        jnp.concatenate([left_high, left_low, left_high], axis=1),
        jnp.concatenate([right_high, right_high, right_low], axis=0),
    )


def inverses_less_eye(couplings, row_at, col_at):
    size = couplings[0].shape[0]
    eye = (row_at == col_at).astype(jnp.float32)
    pairs = row_at // 2 == col_at // 2
    found = [eye - jnp.where(pairs, coupling, 0.0) for coupling in couplings]
    half = 2
    while half < size:
        within = (row_at // (2 * half) == col_at // (2 * half)) & (row_at // half != col_at // half)
        below = [mxu(x, jnp.where(within, c, 0.0)) for x, c in zip(found, couplings)]
        found = [x - mxu(b, x) for x, b in zip(found, below)]
        half *= 2
    found = [x - eye for x in found]
    residue = [-x - c - mxu_wide(c, x) for x, c in zip(found, couplings)]
    return [x + r + mxu(x, r) for x, r in zip(found, residue)]


def layer_kernel(
    ctx_size,
    head_size,
    q_hbm,
    k_hbm,
    v_hbm,
    gate_hbm,
    decay_hbm,
    strength_hbm,
    doc_hbm,
    order_ref,
    weight_ref,
    out_ref,
    decode_ref,
    q_ref,
    k_ref,
    v_ref,
    gate_ref,
    decay_ref,
    strength_ref,
    doc_ref,
    weight,
    opened,
    decay_cols,
    strength_cols,
    decay_rows,
    outbox,
    inbox,
    entering,
    arrived,
    local,
    reader,
    normed,
    final,
    columns,
    partial,
    leaving,
    summands,
    fetch_sem,
    weight_sem,
    map_send,
    map_recv,
    state_send,
    state_recv,
    final_send,
    final_recv,
    column_send,
    column_recv,
    sum_send,
    sum_recv,
):
    me = lax.axis_index("ctx")
    group = lax.axis_index("head")
    rows = q_ref.shape[0]
    key_groups = q_ref.shape[1] // DK
    heads = v_ref.shape[1] // DV
    share = heads // key_groups
    own_rows = rows // head_size
    state_rows = DK // ctx_size
    width = weight.shape[1]
    tiles = width // COLUMN_TILE

    barrier = pltpu.get_barrier_semaphore()
    for away in range(1, ctx_size):
        pl.semaphore_signal(
            barrier, inc=1, device_id=(lax.rem(me + away, ctx_size), group), device_id_type=MESH
        )
    for away in range(1, head_size):
        pl.semaphore_signal(
            barrier, inc=1, device_id=(me, lax.rem(group + away, head_size)), device_id_type=MESH
        )
    fetches = [
        pltpu.make_async_copy(source, held, fetch_sem.at[slot])
        for slot, (source, held) in enumerate(
            (
                (decay_hbm, decay_ref),
                (strength_hbm, strength_ref),
                (doc_hbm, doc_ref),
                (q_hbm, q_ref),
                (k_hbm, k_ref),
                (v_hbm, v_ref),
                (gate_hbm, gate_ref),
            )
        )
    ]
    for fetch in fetches:
        fetch.start()
    weight_fetch = pltpu.make_async_copy(weight_ref, weight, weight_sem)
    weight_fetch.start()

    row_at = lax.broadcasted_iota(jnp.int32, (rows, rows), 0)
    col_at = lax.broadcasted_iota(jnp.int32, (rows, rows), 1)
    causal = row_at >= col_at
    strict = row_at > col_at
    for fetch in fetches[:3]:
        fetch.wait()
    cumulative = jnp.dot(
        decay_ref[...],
        (row_at <= col_at).astype(jnp.float32),
        precision=highest,
        preferred_element_type=jnp.float32,
    )
    for h in range(heads):
        spread = jnp.broadcast_to(cumulative[h : h + 1], (rows, rows))
        decay_cols[h] = spread.T
        decay_rows[h] = spread[0:8]
        strength_cols[h] = jnp.broadcast_to(strength_ref[h : h + 1, :], (rows, rows)).T
    doc_row = doc_ref[...].astype(jnp.float32)
    doc_cols = jnp.broadcast_to(doc_row, (rows, rows)).T
    same_doc = (doc_cols == doc_row) & causal
    first_doc = doc_cols[0:1]
    last_doc = doc_cols[rows - 1 : rows]
    continues = doc_cols == first_doc
    meta_at = lax.broadcasted_iota(jnp.int32, (META_ROWS, rows), 0)

    for fetch in fetches[3:6]:
        fetch.wait()
    pl.semaphore_wait(barrier, ctx_size - 1 + head_size - 1)

    def map_copy(h):
        return pltpu.make_async_remote_copy(
            src_ref=outbox.at[h],
            dst_ref=inbox.at[me],
            send_sem=map_send.at[h],
            recv_sem=map_recv.at[me],
            device_id=(h, group),
            device_id_type=MESH,
        )

    together = 2 if key_groups % 2 == 0 else 1

    def some_heads(turn, _):
        overlaps = []
        for j in range(together):
            kh = lax.rem(me // share + 1 + turn * together + j, key_groups)
            at = pl.ds(pl.multiple_of(kh * DK, DK), DK)
            query_raw = q_ref[:, at]
            key_raw = k_ref[:, at]
            query_wide = query_raw.astype(jnp.float32)
            key_wide = key_raw.astype(jnp.float32)
            query_scale = lax.rsqrt(
                jnp.sum(query_wide * query_wide, axis=-1, keepdims=True) + norm_eps
            ) * DK ** (-0.5)
            key_scale = lax.rsqrt(jnp.sum(key_wide * key_wide, axis=-1, keepdims=True) + norm_eps)
            key_scale_row = jnp.broadcast_to(key_scale, (rows, rows)).T
            raw_across = key_wide.T
            key_overlap = mxu(key_raw, raw_across) * key_scale * key_scale_row
            query_overlap = mxu(query_raw, raw_across) * query_scale * key_scale_row
            parts = (
                query_wide * query_scale,
                key_wide * key_scale,
                raw_across * key_scale_row,
                key_overlap,
                query_overlap,
            )
            overlaps.extend((kh * share + member, parts) for member in range(share))
        mixings, entries, couplings = [], [], []
        for h, parts in overlaps:
            decay = decay_cols[h]
            mixing = jnp.where(
                same_doc, jnp.exp(jnp.minimum(decay - decay_rows[h][0:1], 0.0)), 0.0
            )
            mixings.append(mixing)
            entries.append(jnp.where(continues, jnp.exp(decay), 0.0))
            couplings.append(jnp.where(strict, strength_cols[h] * mixing * parts[3], 0.0))
        solved = inverses_less_eye(couplings, row_at, col_at)
        sides = []
        for (h, parts), entry in zip(overlaps, entries):
            value_at = pl.ds(pl.multiple_of(h * DV, DV), DV)
            strength = strength_cols[h]
            value_part = v_ref[:, value_at].astype(jnp.float32)
            sides.append(
                jnp.concatenate([strength * entry * parts[1], strength * value_part], axis=1)
            )
        sides = [side + mxu_wide(x, side) for x, side in zip(solved, sides)]
        for (h, parts), entry, mixing, side in zip(overlaps, entries, mixings, sides):
            moved = mxu_wide(parts[2] * mixing[rows - 1 : rows], side)
            outbox[h, 0:DK, :] = (-moved[:, :DK]).astype(jnp.bfloat16)
            outbox[h, DK : 2 * DK, :] = moved[:, DK:].astype(jnp.bfloat16)
            kept = entry[rows - 1 : rows]
            kept_high = kept.astype(jnp.bfloat16).astype(jnp.float32)
            meta = jnp.where(
                meta_at == 0,
                kept_high,
                jnp.where(
                    meta_at == 1, kept - kept_high, jnp.where(meta_at == 2, first_doc, last_doc)
                ),
            )
            outbox[h, 2 * DK : 2 * DK + META_ROWS, :] = meta.astype(jnp.bfloat16)
        for h, _ in overlaps:

            @pl.when(h != me)
            def _():
                map_copy(h).start()

            @pl.when(h == me)
            def _():
                inbox[me] = outbox[me]

        for (h, parts), entry, mixing, side in zip(overlaps, entries, mixings, sides):
            seen = mxu_wide(mixing * parts[4], side)
            local[h] = seen[:, DK:]
            reader[h] = entry * parts[0] - seen[:, :DK]

        return 0

    lax.fori_loop(0, key_groups // together, some_heads, 0)

    fetches[6].wait()
    gate = gate_ref[...].astype(jnp.float32)
    opened[...] = gate / (1.0 + jnp.exp(-gate))

    def state_copy(i):
        return pltpu.make_async_remote_copy(
            src_ref=entering.at[i],
            dst_ref=arrived.at[me],
            send_sem=state_send.at[i],
            recv_sem=state_recv.at[me],
            device_id=(i, group),
            device_id_type=MESH,
        )

    def landed(buffer, slot, send, recv):
        return pltpu.make_async_remote_copy(
            src_ref=buffer.at[slot],
            dst_ref=buffer.at[slot],
            send_sem=send.at[slot],
            recv_sem=recv.at[slot],
            device_id=(slot, group),
            device_id_type=MESH,
        )

    state = jnp.zeros((DK, DV), jnp.float32)
    doc_before = None
    for i in range(ctx_size):

        @pl.when(me != i)
        def _():
            landed(inbox, i, map_send, map_recv).wait_recv()

        meta = inbox[i, 2 * DK : 2 * DK + META_ROWS, :].astype(jnp.float32)
        if i > 0:
            state = jnp.where(meta[2:3] == doc_before, state, 0.0)
        doc_before = meta[3:4]
        state_low = state.astype(jnp.bfloat16)
        entering[i] = state_low

        @pl.when(me != i)
        def _():
            state_copy(i).start()

        @pl.when(me == i)
        def _():
            arrived[i] = entering[i]

        added = inbox[i, DK : 2 * DK, :].astype(jnp.float32)
        state = (meta[0:1] + meta[1:2]) * state + mxu(inbox[i, 0:DK, :], state_low) + added
    final[...] = state

    head_here = group * heads + me

    def final_copy(c):
        return pltpu.make_async_remote_copy(
            src_ref=final.at[pl.ds(pl.multiple_of(c * state_rows, state_rows), state_rows)],
            dst_ref=columns.at[head_here],
            send_sem=final_send.at[c],
            recv_sem=final_recv.at[me],
            device_id=(c, group),
            device_id_type=MESH,
        )

    for away in range(1, ctx_size):
        final_copy(lax.rem(me + away, ctx_size)).start()
    columns[head_here] = final[pl.ds(pl.multiple_of(me * state_rows, state_rows), state_rows)]

    for h in range(heads):

        @pl.when(me != h)
        def _():
            landed(arrived, h, state_send, state_recv).wait_recv()

    for h in range(heads):
        at = slice(h * DV, (h + 1) * DV)
        attention = local[h] + mxu_wide_left(reader[h], arrived[h])
        mean_square = jnp.mean(attention * attention, axis=-1, keepdims=True)
        gated = attention * lax.rsqrt(mean_square + norm_eps) * opened[:, at]
        normed[:, at] = gated.astype(jnp.bfloat16)

    weight_fetch.wait()

    def sum_copy(tile, away):
        peer = lax.rem(group + away, head_size)
        return pltpu.make_async_remote_copy(
            src_ref=leaving.at[tile, pl.ds(pl.multiple_of(peer * own_rows, own_rows), own_rows)],
            dst_ref=summands.at[tile, away],
            send_sem=sum_send.at[tile, away],
            recv_sem=sum_recv.at[tile, away],
            device_id=(me, peer),
            device_id_type=MESH,
        )

    for tile in range(tiles):
        at = slice(tile * COLUMN_TILE, (tile + 1) * COLUMN_TILE)
        product_here = jnp.dot(normed[...], weight[:, at], preferred_element_type=jnp.float32)
        partial[:, at] = product_here
        leaving[tile] = product_here.astype(jnp.bfloat16)
        for away in range(1, head_size):
            sum_copy(tile, away).start()

    for away in range(1, ctx_size):
        source = lax.rem(me + away, ctx_size)
        pltpu.make_async_remote_copy(
            src_ref=columns.at[group * heads + source],
            dst_ref=columns.at[group * heads + source],
            send_sem=final_send.at[source],
            recv_sem=final_recv.at[source],
            device_id=(source, group),
            device_id_type=MESH,
        ).wait_recv()

    def column_copy(peer, block, slot):
        return pltpu.make_async_remote_copy(
            src_ref=columns.at[pl.ds(block * heads, heads)],
            dst_ref=columns.at[pl.ds(block * heads, heads)],
            send_sem=column_send.at[slot],
            recv_sem=column_recv.at[slot],
            device_id=(me, peer),
            device_id_type=MESH,
        )

    for away in range(1, head_size):
        column_copy(lax.rem(group + away, head_size), group, away).start()

    for tile in range(tiles):
        at = slice(tile * COLUMN_TILE, (tile + 1) * COLUMN_TILE)
        total = partial[pl.ds(pl.multiple_of(group * own_rows, own_rows), own_rows), at]
        for away in range(1, head_size):
            sum_copy(tile, away).wait_recv()
            total = total + summands[tile, away].astype(jnp.float32)
        out_ref[:, at] = total.astype(jnp.bfloat16)

    for away in range(1, head_size):
        source = lax.rem(group + head_size - away, head_size)
        column_copy(source, source, away).wait_recv()
    for slot in range(heads):
        chosen = columns[order_ref[group * heads + slot]]
        for r in range(state_rows):
            decode_ref[slot : slot + 1, r * DV : (r + 1) * DV] = chosen[r : r + 1]

    for away in range(1, ctx_size):
        other = lax.rem(me + away, ctx_size)
        map_copy(other).wait_send()
        state_copy(other).wait_send()
        final_copy(other).wait_send()
    for away in range(1, head_size):
        column_copy(lax.rem(group + away, head_size), group, away).wait_send()
        for tile in range(tiles):
            sum_copy(tile, away).wait_send()


def head_owner(
    queries, keys, values, out_gate, log_decay, write_strength, segment_ids, head_order, out_weight
):
    rows = queries.shape[0]
    heads = values.shape[1] // DV
    ctx_size, head_size = lax.axis_size("ctx"), lax.axis_size("head")
    width = out_weight.shape[1]
    tiles = width // COLUMN_TILE
    own_rows = rows // head_size
    state_rows = DK // ctx_size
    f32, bf16 = jnp.float32, jnp.bfloat16
    dma = pltpu.SemaphoreType.DMA
    vmem = pl.BlockSpec(memory_space=pltpu.VMEM)
    hbm = pl.BlockSpec(memory_space=pltpu.HBM)
    return pl.pallas_call(
        functools.partial(layer_kernel, ctx_size, head_size),
        out_shape=(
            jax.ShapeDtypeStruct((own_rows, width), bf16),
            jax.ShapeDtypeStruct((heads, state_rows * DV), f32),
        ),
        in_specs=[hbm] * 7 + [pl.BlockSpec(memory_space=pltpu.SMEM), hbm],
        out_specs=(vmem, vmem),
        scratch_shapes=[
            pltpu.VMEM(queries.shape, bf16),
            pltpu.VMEM(keys.shape, bf16),
            pltpu.VMEM(values.shape, bf16),
            pltpu.VMEM(out_gate.shape, bf16),
            pltpu.VMEM((heads, rows), f32),
            pltpu.VMEM((heads, rows), f32),
            pltpu.VMEM((1, rows), jnp.int32),
            pltpu.VMEM(out_weight.shape, bf16),
            pltpu.VMEM((rows, heads * DV), f32),
            pltpu.VMEM((heads, rows, rows), f32),
            pltpu.VMEM((heads, rows, rows), f32),
            pltpu.VMEM((heads, 8, rows), f32),
            pltpu.VMEM((heads, 2 * DK + META_ROWS, DV), bf16),
            pltpu.VMEM((ctx_size, 2 * DK + META_ROWS, DV), bf16),
            pltpu.VMEM((ctx_size, DK, DV), bf16),
            pltpu.VMEM((heads, DK, DV), bf16),
            pltpu.VMEM((heads, rows, DV), f32),
            pltpu.VMEM((heads, rows, DK), f32),
            pltpu.VMEM((rows, heads * DV), bf16),
            pltpu.VMEM((DK, DV), f32),
            pltpu.VMEM((head_size * heads, state_rows, DV), f32),
            pltpu.VMEM((rows, width), f32),
            pltpu.VMEM((tiles, rows, COLUMN_TILE), bf16),
            pltpu.VMEM((tiles, head_size, own_rows, COLUMN_TILE), bf16),
            dma((7,)),
            dma,
            dma((heads,)),
            dma((ctx_size,)),
            dma((ctx_size,)),
            dma((heads,)),
            dma((ctx_size,)),
            dma((ctx_size,)),
            dma((head_size,)),
            dma((head_size,)),
            dma((tiles, head_size)),
            dma((tiles, head_size)),
        ],
        compiler_params=pltpu.CompilerParams(
            collective_id=0, has_side_effects=True, vmem_limit_bytes=56 * 1024 * 1024
        ),
    )(
        queries,
        keys,
        values,
        out_gate,
        log_decay.T,
        write_strength.T,
        segment_ids.reshape(1, rows),
        head_order,
        out_weight,
    )


def per_device(queries, keys, values, *rest):
    heads = values.shape[1] // DV
    one_owner_per_head = heads == lax.axis_size("ctx") and queries.shape[0] == DK
    form = head_owner if one_owner_per_head else gathered_prefix
    return form(queries, keys, values, *rest)


def solution(mesh):
    in_specs = (
        P("ctx", "head"),
        P("ctx", "head"),
        P("ctx", "head"),
        P("ctx", "head"),
        P("ctx", "head"),
        P("ctx", "head"),
        P("ctx"),
        P(),
        P("head", None),
    )
    out_specs = (P(("ctx", "head"), None), P("head", "ctx"))
    return jax.shard_map(
        per_device, mesh=mesh, in_specs=in_specs, out_specs=out_specs, check_vma=False
    )
```

```python
import functools

import jax
import jax.numpy as jnp
from jax import lax
from jax.experimental import pallas as pl
from jax.experimental.pallas import tpu as pltpu
from jax.sharding import PartitionSpec as P

DK = 128
DV = 128
BLOCK = 64


highest = lax.Precision.HIGHEST
norm_eps = 1e-06


def prefix(x, axis, combine, identity):
    peers, index = (lax.axis_size(axis), lax.axis_index(axis))
    everything = jax.tree.map(lambda part: lax.all_gather(part, axis), x)
    start = jax.tree.map(
        lambda part, zero: jnp.broadcast_to(jnp.asarray(zero, part.dtype), part.shape), x, identity
    )

    def step(k, before):
        reached = k < index
        new = combine(before, jax.tree.map(lambda part: part[k], everything))
        return jax.tree.map(lambda a, b: jnp.where(reached, a, b), new, before)

    return lax.fori_loop(0, peers, step, start)


def product(form, left, right):
    return jnp.einsum(form, left, right, precision=highest)


def unit_rows(raw_rows, scaling):
    widened = raw_rows.astype(jnp.float32)
    return (
        widened * lax.rsqrt(jnp.sum(widened * widened, axis=-1, keepdims=True) + norm_eps) * scaling
    )


def gated_norm(attention, gate_rows):
    mean_square = jnp.mean(attention * attention, axis=-1, keepdims=True)
    gated = (
        attention * lax.rsqrt(mean_square + norm_eps) * jax.nn.silu(gate_rows.astype(jnp.float32))
    )
    return gated.astype(jnp.bfloat16)


def inverse_unit_lower(coupling):
    block_size = coupling.shape[-1]
    identity_matrix = jnp.eye(block_size, dtype=jnp.float32)
    inverse = identity_matrix - coupling
    squared = coupling
    for doubling in range(block_size.bit_length() - 2):
        squared = product("...ij,...jk->...ik", squared, squared)
        inverse = product("...ij,...jk->...ik", inverse, identity_matrix + squared)
    return inverse


def block_parts(query_part, key_part, value_part, decay_rows, strength_rows, doc_rows, doc_before):
    block_size = doc_rows.shape[-1]
    token_positions = jnp.arange(block_size)
    causal = token_positions[:, None] >= token_positions[None, :]
    strict = token_positions[:, None] > token_positions[None, :]
    same_doc = (doc_rows[..., :, None] == doc_rows[..., None, :]) & causal
    continues = doc_rows == doc_before[..., None]
    cumulative = jnp.cumsum(decay_rows, axis=-1)
    decay_gap = cumulative[..., :, None] - cumulative[..., None, :]
    mixing = jnp.where(same_doc[..., None, :, :], jnp.exp(jnp.minimum(decay_gap, 0.0)), 0.0)
    entry_decay = jnp.where(continues[..., None, :], jnp.exp(cumulative), 0.0)
    key_intersection = product("...id,...jd->...ij", key_part, key_part)
    coupling = jnp.where(strict, strength_rows[..., :, None] * mixing * key_intersection, 0.0)
    inverse = inverse_unit_lower(coupling)
    weighted = product(
        "...ij,...jd->...id", inverse, (strength_rows * entry_decay)[..., None] * key_part
    )
    pseudo_values = product("...ij,...jd->...id", inverse, strength_rows[..., None] * value_part)
    masked_scores = mixing * product("...id,...jd->...ij", query_part, key_part)
    local_out = product("...ij,...jd->...id", masked_scores, pseudo_values)
    state_read = entry_decay[..., None] * query_part - product(
        "...ij,...jd->...id", masked_scores, weighted
    )
    last_keys = mixing[..., -1, :, None] * key_part
    identity_map = jnp.eye(key_part.shape[-1], dtype=jnp.float32)
    transition = entry_decay[..., -1, None, None] * identity_map - product(
        "...jd,...je->...de", last_keys, weighted
    )
    written = product("...jd,...je->...de", last_keys, pseudo_values)
    return (local_out, state_read, transition, written)


def combine_spans(earlier, later):
    linked = jnp.where((earlier[3] < 0) | (later[2] < 0) | (earlier[3] == later[2]), 1.0, 0.0)
    through = linked * product("hde,hef->hdf", later[0], earlier[0])
    reached = linked * product("hde,hef->hdf", later[0], earlier[1]) + later[1]
    first_doc = jnp.where(earlier[2] >= 0, earlier[2], later[2])
    last_doc = jnp.where(later[3] >= 0, later[3], earlier[3])
    return (through, reached, first_doc, last_doc)


def gathered_prefix(
    queries, keys, values, out_gate, log_decay, write_strength, segment_ids, head_order, out_weight
):
    tok_rows = queries.shape[0]
    heads_here = values.shape[1] // DV
    key_groups = queries.shape[1] // DK
    group_size = heads_here // key_groups
    blocks = tok_rows // BLOCK

    def head_major(raw_rows, scaling):
        unit_part = unit_rows(raw_rows.reshape(blocks, BLOCK, key_groups, DK), scaling)
        return jnp.repeat(unit_part, group_size, axis=2).transpose(0, 2, 1, 3)

    query_part = head_major(queries, DK ** (-0.5))
    key_part = head_major(keys, 1.0)
    value_part = (
        values.reshape(blocks, BLOCK, heads_here, DV).astype(jnp.float32).transpose(0, 2, 1, 3)
    )
    decay_rows = log_decay.reshape(blocks, BLOCK, heads_here).transpose(0, 2, 1)
    strength_rows = write_strength.reshape(blocks, BLOCK, heads_here).transpose(0, 2, 1)
    doc_blocks = segment_ids.reshape(blocks, BLOCK)
    doc_before = jnp.concatenate([doc_blocks[:1, 0], doc_blocks[:-1, -1]])
    local_out, state_read, transition, written = block_parts(
        query_part, key_part, value_part, decay_rows, strength_rows, doc_blocks, doc_before
    )
    identity_map = jnp.broadcast_to(jnp.eye(DK, dtype=jnp.float32), (heads_here, DK, DK))
    zero_state = jnp.zeros((heads_here, DK, DV), jnp.float32)

    def compose_keep(carried, pieces):
        through, reached = carried
        step_map, step_add = pieces
        updated = (
            product("hde,hef->hdf", step_map, through),
            product("hde,hef->hdf", step_map, reached) + step_add,
        )
        return (updated, carried)

    (whole_map, whole_add), (prefix_maps, prefix_states) = lax.scan(
        compose_keep, (identity_map, zero_state), (transition, written)
    )
    early_out = local_out + product("chid,chde->chie", state_read, prefix_states)
    first_doc = doc_blocks[0, 0].astype(jnp.float32)
    last_doc = doc_blocks[-1, -1].astype(jnp.float32)
    identity = (identity_map, zero_state, jnp.float32(-1.0), jnp.float32(-1.0))
    before = prefix((whole_map, whole_add, first_doc, last_doc), "ctx", combine_spans, identity)
    linked = jnp.where((before[3] < 0) | (before[3] == first_doc), 1.0, 0.0)
    incoming = linked * before[1]
    reach = product("chde,hef->chdf", prefix_maps, incoming)
    attention = early_out + product("chid,chde->chie", state_read, reach)
    final_state = product("hde,hef->hdf", whole_map, incoming) + whole_add
    tokens_major = attention.transpose(0, 2, 1, 3).reshape(tok_rows, heads_here, DV)
    normed = gated_norm(tokens_major, out_gate.reshape(tok_rows, heads_here, DV)).reshape(
        tok_rows, heads_here * DV
    )
    summed = lax.psum_scatter(
        jnp.dot(normed, out_weight, preferred_element_type=jnp.float32),
        "head",
        scatter_dimension=0,
        tiled=True,
    )
    layer_out = summed.astype(jnp.bfloat16)
    groups = lax.axis_size("ctx")
    is_last = jnp.where(lax.axis_index("ctx") == groups - 1, 1.0, 0.0).astype(jnp.float32)
    own_columns = lax.psum_scatter(
        final_state.reshape(heads_here, DK * DV) * is_last, "ctx", scatter_dimension=1, tiled=True
    )
    every_head = lax.all_gather(own_columns, "head", axis=0, tiled=True)
    order_here = lax.dynamic_slice_in_dim(
        head_order, lax.axis_index("head") * heads_here, heads_here, 0
    )
    selector = (
        order_here[:, None] == jnp.arange(every_head.shape[0], dtype=jnp.int32)[None, :]
    ).astype(jnp.float32)
    decode_states = product("jh,hw->jw", selector, every_head)
    return (layer_out, decode_states)


MESH = pl.DeviceIdType.MESH
COLUMN_TILE = 512
META_ROWS = 16


def mxu(left, right):
    return jnp.dot(
        left.astype(jnp.bfloat16), right.astype(jnp.bfloat16), preferred_element_type=jnp.float32
    )


def split(wide):
    high = wide.astype(jnp.bfloat16)
    return high, (wide - high.astype(jnp.float32)).astype(jnp.bfloat16)


def mxu_wide_left(left, right):
    high, low = split(left)
    right = right.astype(jnp.bfloat16)
    return mxu(jnp.concatenate([high, low], axis=1), jnp.concatenate([right, right], axis=0))


def mxu_wide(left, right):
    left_high, left_low = split(left)
    right_high, right_low = split(right)
    return mxu(
        jnp.concatenate([left_high, left_low, left_high], axis=1),
        jnp.concatenate([right_high, right_high, right_low], axis=0),
    )


def inverses_less_eye(couplings, row_at, col_at):
    size = couplings[0].shape[0]
    eye = (row_at == col_at).astype(jnp.float32)
    pairs = row_at // 2 == col_at // 2
    found = [eye - jnp.where(pairs, coupling, 0.0) for coupling in couplings]
    half = 2
    while 2 * half < size:
        within = (row_at // (2 * half) == col_at // (2 * half)) & (row_at // half != col_at // half)
        below = [mxu(x, jnp.where(within, c, 0.0)) for x, c in zip(found, couplings)]
        found = [x - mxu(b, x) for x, b in zip(found, below)]
        half *= 2
    found = [x - eye for x in found]
    residue = [-x - c - mxu_wide(c, x) for x, c in zip(found, couplings)]
    return [x + r + mxu_wide(x, r) for x, r in zip(found, residue)]


def layer_kernel(
    ctx_size,
    head_size,
    q_hbm,
    k_hbm,
    v_hbm,
    gate_hbm,
    decay_hbm,
    strength_hbm,
    doc_hbm,
    order_ref,
    weight_ref,
    out_ref,
    decode_ref,
    q_ref,
    k_ref,
    v_ref,
    gate_ref,
    decay_ref,
    strength_ref,
    doc_ref,
    weight,
    opened,
    decay_cols,
    strength_cols,
    decay_rows,
    outbox,
    inbox,
    entering,
    arrived,
    local,
    reader,
    normed,
    final,
    columns,
    partial,
    paired,
    leaving,
    summands,
    fetch_sem,
    weight_sem,
    map_send,
    map_recv,
    state_send,
    state_recv,
    final_send,
    final_recv,
    column_send,
    column_recv,
    mate_send,
    mate_recv,
    sum_send,
    sum_recv,
):
    me = lax.axis_index("ctx")
    group = lax.axis_index("head")
    rows = q_ref.shape[0]
    key_groups = q_ref.shape[1] // DK
    heads = v_ref.shape[1] // DV
    share = heads // key_groups
    own_rows = rows // head_size
    state_rows = DK // ctx_size
    width = weight.shape[1]
    tiles = width // COLUMN_TILE

    barrier = pltpu.get_barrier_semaphore()
    for away in range(1, ctx_size):
        pl.semaphore_signal(
            barrier, inc=1, device_id=(lax.rem(me + away, ctx_size), group), device_id_type=MESH
        )
    for away in range(1, head_size):
        pl.semaphore_signal(
            barrier, inc=1, device_id=(me, lax.rem(group + away, head_size)), device_id_type=MESH
        )
    fetches = [
        pltpu.make_async_copy(source, held, fetch_sem.at[slot])
        for slot, (source, held) in enumerate(
            (
                (decay_hbm, decay_ref),
                (strength_hbm, strength_ref),
                (doc_hbm, doc_ref),
                (q_hbm, q_ref),
                (k_hbm, k_ref),
                (v_hbm, v_ref),
                (gate_hbm, gate_ref),
            )
        )
    ]
    for fetch in fetches:
        fetch.start()
    weight_fetch = pltpu.make_async_copy(weight_ref, weight, weight_sem)
    weight_fetch.start()

    row_at = lax.broadcasted_iota(jnp.int32, (rows, rows), 0)
    col_at = lax.broadcasted_iota(jnp.int32, (rows, rows), 1)
    causal = row_at >= col_at
    strict = row_at > col_at
    for fetch in fetches[:3]:
        fetch.wait()
    cumulative = jnp.dot(
        decay_ref[...],
        (row_at <= col_at).astype(jnp.float32),
        precision=highest,
        preferred_element_type=jnp.float32,
    )
    for h in range(heads):
        spread = jnp.broadcast_to(cumulative[h : h + 1], (rows, rows))
        decay_cols[h] = spread.T
        decay_rows[h] = spread[0:8]
        strength_cols[h] = jnp.broadcast_to(strength_ref[h : h + 1, :], (rows, rows)).T
    doc_row = doc_ref[...].astype(jnp.float32)
    doc_cols = jnp.broadcast_to(doc_row, (rows, rows)).T
    same_doc = (doc_cols == doc_row) & causal
    first_doc = doc_cols[0:1]
    last_doc = doc_cols[rows - 1 : rows]
    continues = doc_cols == first_doc
    meta_at = lax.broadcasted_iota(jnp.int32, (META_ROWS, rows), 0)

    for fetch in fetches[3:6]:
        fetch.wait()
    pl.semaphore_wait(barrier, ctx_size - 1 + head_size - 1)

    def map_copy(h):
        return pltpu.make_async_remote_copy(
            src_ref=outbox.at[h],
            dst_ref=inbox.at[me],
            send_sem=map_send.at[h],
            recv_sem=map_recv.at[me],
            device_id=(h, group),
            device_id_type=MESH,
        )

    together = 2 if key_groups % 2 == 0 else 1

    def some_heads(turn):
        overlaps = []
        for j in range(together):
            kh = lax.rem(me // share + 1 + turn * together + j, key_groups)
            at = pl.ds(pl.multiple_of(kh * DK, DK), DK)
            query_raw = q_ref[:, at]
            key_raw = k_ref[:, at]
            query_wide = query_raw.astype(jnp.float32)
            key_wide = key_raw.astype(jnp.float32)
            query_scale = lax.rsqrt(
                jnp.sum(query_wide * query_wide, axis=-1, keepdims=True) + norm_eps
            ) * DK ** (-0.5)
            key_scale = lax.rsqrt(jnp.sum(key_wide * key_wide, axis=-1, keepdims=True) + norm_eps)
            key_scale_row = jnp.broadcast_to(key_scale, (rows, rows)).T
            raw_across = key_wide.T
            key_overlap = mxu(key_raw, raw_across) * key_scale * key_scale_row
            query_overlap = mxu(query_raw, raw_across) * query_scale * key_scale_row
            parts = (
                query_wide * query_scale,
                key_wide * key_scale,
                raw_across * key_scale_row,
                key_overlap,
                query_overlap,
            )
            overlaps.extend((kh * share + member, parts) for member in range(share))
        mixings, entries, couplings = [], [], []
        for h, parts in overlaps:
            decay = decay_cols[h]
            mixing = jnp.where(
                same_doc, jnp.exp(jnp.minimum(decay - decay_rows[h][0:1], 0.0)), 0.0
            )
            mixings.append(mixing)
            entries.append(jnp.where(continues, jnp.exp(decay), 0.0))
            couplings.append(jnp.where(strict, strength_cols[h] * mixing * parts[3], 0.0))
        solved = inverses_less_eye(couplings, row_at, col_at)
        sides = []
        for (h, parts), entry in zip(overlaps, entries):
            value_at = pl.ds(pl.multiple_of(h * DV, DV), DV)
            strength = strength_cols[h]
            value_part = v_ref[:, value_at].astype(jnp.float32)
            sides.append(
                jnp.concatenate([strength * entry * parts[1], strength * value_part], axis=1)
            )
        sides = [side + mxu_wide(x, side) for x, side in zip(solved, sides)]
        for (h, parts), entry, mixing, side in zip(overlaps, entries, mixings, sides):
            moved = mxu_wide(parts[2] * mixing[rows - 1 : rows], side)
            outbox[h, 0:DK, :] = (-moved[:, :DK]).astype(jnp.bfloat16)
            outbox[h, DK : 2 * DK, :] = moved[:, DK:].astype(jnp.bfloat16)
            kept = entry[rows - 1 : rows]
            kept_high = kept.astype(jnp.bfloat16).astype(jnp.float32)
            meta = jnp.where(
                meta_at == 0,
                kept_high,
                jnp.where(
                    meta_at == 1, kept - kept_high, jnp.where(meta_at == 2, first_doc, last_doc)
                ),
            )
            outbox[h, 2 * DK : 2 * DK + META_ROWS, :] = meta.astype(jnp.bfloat16)
        last_turn = turn == key_groups // together - 1
        for h, _ in overlaps[: len(overlaps) - share if last_turn else None]:
            map_copy(h).start()
        if last_turn:
            for away in range(1, share):
                map_copy(me // share * share + lax.rem(me + away, share)).start()
            inbox[me] = outbox[me]

        for (h, parts), entry, mixing, side in zip(overlaps, entries, mixings, sides):
            seen = mxu_wide(mixing * parts[4], side)
            local[h] = seen[:, DK:]
            reader[h] = entry * parts[0] - seen[:, :DK]

    for turn in range(key_groups // together):
        some_heads(turn)

    fetches[6].wait()
    gate = gate_ref[...].astype(jnp.float32)
    opened[...] = gate / (1.0 + jnp.exp(-gate))

    def state_copy(i):
        return pltpu.make_async_remote_copy(
            src_ref=entering.at[i],
            dst_ref=arrived.at[me],
            send_sem=state_send.at[i],
            recv_sem=state_recv.at[me],
            device_id=(i, group),
            device_id_type=MESH,
        )

    def landed(buffer, slot, send, recv):
        return pltpu.make_async_remote_copy(
            src_ref=buffer.at[slot],
            dst_ref=buffer.at[slot],
            send_sem=send.at[slot],
            recv_sem=recv.at[slot],
            device_id=(slot, group),
            device_id_type=MESH,
        )

    state = jnp.zeros((DK, DV), jnp.float32)
    doc_before = None
    for i in range(ctx_size):

        @pl.when(me != i)
        def _():
            landed(inbox, i, map_send, map_recv).wait_recv()

        meta = inbox[i, 2 * DK : 2 * DK + META_ROWS, :].astype(jnp.float32)
        if i > 0:
            state = jnp.where(meta[2:3] == doc_before, state, 0.0)
        doc_before = meta[3:4]
        state_low = state.astype(jnp.bfloat16)
        if i == 0:

            @pl.when(me == 0)
            def _():
                arrived[...] = jnp.zeros_like(arrived)

        else:
            entering[i] = state_low

            @pl.when(me != i)
            def _():
                state_copy(i).start()

            @pl.when(me == i)
            def _():
                arrived[i] = entering[i]

        added = inbox[i, DK : 2 * DK, :].astype(jnp.float32)
        state = (meta[0:1] + meta[1:2]) * state + mxu(inbox[i, 0:DK, :], state_low) + added
    final[...] = state

    head_here = group * heads + me

    def final_copy(c):
        return pltpu.make_async_remote_copy(
            src_ref=final.at[pl.ds(pl.multiple_of(c * state_rows, state_rows), state_rows)],
            dst_ref=columns.at[head_here],
            send_sem=final_send.at[c],
            recv_sem=final_recv.at[me],
            device_id=(c, group),
            device_id_type=MESH,
        )

    for away in range(1, ctx_size):
        final_copy(lax.rem(me + away, ctx_size)).start()
    columns[head_here] = final[pl.ds(pl.multiple_of(me * state_rows, state_rows), state_rows)]

    for h in range(heads):

        @pl.when((me != h) & (me != 0))
        def _():
            landed(arrived, h, state_send, state_recv).wait_recv()

    for h in range(heads):
        at = slice(h * DV, (h + 1) * DV)
        attention = local[h] + mxu_wide_left(reader[h], arrived[h])
        mean_square = jnp.mean(attention * attention, axis=-1, keepdims=True)
        gated = attention * lax.rsqrt(mean_square + norm_eps) * opened[:, at]
        normed[:, at] = gated.astype(jnp.bfloat16)

    weight_fetch.wait()

    half = head_size // 2
    side, place_here = lax.rem(group, 2), group // 2
    mate = 2 * place_here + 1 - side

    def mate_copy(tile, place):
        return pltpu.make_async_remote_copy(
            src_ref=partial.at[tile, 2 * place + 1 - side],
            dst_ref=paired.at[tile, place],
            send_sem=mate_send.at[tile, place],
            recv_sem=mate_recv.at[tile, place],
            device_id=(me, mate),
            device_id_type=MESH,
        )

    def sum_copy(tile, away):
        return pltpu.make_async_remote_copy(
            src_ref=leaving.at[tile, away],
            dst_ref=summands.at[tile, away],
            send_sem=sum_send.at[tile, away],
            recv_sem=sum_recv.at[tile, away],
            device_id=(me, 2 * lax.rem(place_here + away, half) + side),
            device_id_type=MESH,
        )

    def pass_on(tile):
        for place in range(half):
            mate_copy(tile, place).wait_recv()
        for away in range(1, half):
            place = lax.rem(place_here + away, half)
            pair_sum = partial[tile, 2 * place + side] + paired[tile, place]
            leaving[tile, away] = pair_sum.astype(jnp.bfloat16)
            sum_copy(tile, away).start()

    for tile in range(tiles):
        at = slice(tile * COLUMN_TILE, (tile + 1) * COLUMN_TILE)
        product_here = jnp.dot(normed[...], weight[:, at], preferred_element_type=jnp.float32)
        partial[tile] = product_here.reshape(head_size, own_rows, COLUMN_TILE)
        for place in range(half):
            mate_copy(tile, place).start()
        if tile > 0:
            pass_on(tile - 1)
    pass_on(tiles - 1)

    for away in range(1, ctx_size):
        source = lax.rem(me + away, ctx_size)
        pltpu.make_async_remote_copy(
            src_ref=columns.at[group * heads + source],
            dst_ref=columns.at[group * heads + source],
            send_sem=final_send.at[source],
            recv_sem=final_recv.at[source],
            device_id=(source, group),
            device_id_type=MESH,
        ).wait_recv()

    def column_copy(peer, block, slot):
        return pltpu.make_async_remote_copy(
            src_ref=columns.at[pl.ds(block * heads, heads)],
            dst_ref=columns.at[pl.ds(block * heads, heads)],
            send_sem=column_send.at[slot],
            recv_sem=column_recv.at[slot],
            device_id=(me, peer),
            device_id_type=MESH,
        )

    for away in range(1, head_size):
        column_copy(lax.rem(group + away, head_size), group, away).start()

    for tile in range(tiles):
        at = slice(tile * COLUMN_TILE, (tile + 1) * COLUMN_TILE)
        total = partial[tile, group] + paired[tile, place_here]
        for away in range(1, half):
            sum_copy(tile, away).wait_recv()
            total = total + summands[tile, away].astype(jnp.float32)
        out_ref[:, at] = total.astype(jnp.bfloat16)

    for away in range(1, head_size):
        source = lax.rem(group + head_size - away, head_size)
        column_copy(source, source, away).wait_recv()
    for slot in range(heads):
        chosen = columns[order_ref[group * heads + slot]]
        for r in range(state_rows):
            decode_ref[slot : slot + 1, r * DV : (r + 1) * DV] = chosen[r : r + 1]

    for away in range(1, ctx_size):
        other = lax.rem(me + away, ctx_size)
        map_copy(other).wait_send()
        final_copy(other).wait_send()
    for i in range(1, ctx_size):

        @pl.when(me != i)
        def _():
            state_copy(i).wait_send()

    for away in range(1, head_size):
        column_copy(lax.rem(group + away, head_size), group, away).wait_send()
    for tile in range(tiles):
        for place in range(half):
            mate_copy(tile, place).wait_send()
        for away in range(1, half):
            sum_copy(tile, away).wait_send()


def head_owner(
    queries, keys, values, out_gate, log_decay, write_strength, segment_ids, head_order, out_weight
):
    rows = queries.shape[0]
    heads = values.shape[1] // DV
    ctx_size, head_size = lax.axis_size("ctx"), lax.axis_size("head")
    width = out_weight.shape[1]
    tiles = width // COLUMN_TILE
    own_rows = rows // head_size
    half = head_size // 2
    state_rows = DK // ctx_size
    f32, bf16 = jnp.float32, jnp.bfloat16
    dma = pltpu.SemaphoreType.DMA
    vmem = pl.BlockSpec(memory_space=pltpu.VMEM)
    hbm = pl.BlockSpec(memory_space=pltpu.HBM)
    return pl.pallas_call(
        functools.partial(layer_kernel, ctx_size, head_size),
        out_shape=(
            jax.ShapeDtypeStruct((own_rows, width), bf16),
            jax.ShapeDtypeStruct((heads, state_rows * DV), f32),
        ),
        in_specs=[hbm] * 7 + [pl.BlockSpec(memory_space=pltpu.SMEM), hbm],
        out_specs=(vmem, vmem),
        scratch_shapes=[
            pltpu.VMEM(queries.shape, bf16),
            pltpu.VMEM(keys.shape, bf16),
            pltpu.VMEM(values.shape, bf16),
            pltpu.VMEM(out_gate.shape, bf16),
            pltpu.VMEM((heads, rows), f32),
            pltpu.VMEM((heads, rows), f32),
            pltpu.VMEM((1, rows), jnp.int32),
            pltpu.VMEM(out_weight.shape, bf16),
            pltpu.VMEM((rows, heads * DV), f32),
            pltpu.VMEM((heads, rows, rows), f32),
            pltpu.VMEM((heads, rows, rows), f32),
            pltpu.VMEM((heads, 8, rows), f32),
            pltpu.VMEM((heads, 2 * DK + META_ROWS, DV), bf16),
            pltpu.VMEM((ctx_size, 2 * DK + META_ROWS, DV), bf16),
            pltpu.VMEM((ctx_size, DK, DV), bf16),
            pltpu.VMEM((heads, DK, DV), bf16),
            pltpu.VMEM((heads, rows, DV), f32),
            pltpu.VMEM((heads, rows, DK), f32),
            pltpu.VMEM((rows, heads * DV), bf16),
            pltpu.VMEM((DK, DV), f32),
            pltpu.VMEM((head_size * heads, state_rows, DV), f32),
            pltpu.VMEM((tiles, head_size, own_rows, COLUMN_TILE), f32),
            pltpu.VMEM((tiles, half, own_rows, COLUMN_TILE), f32),
            pltpu.VMEM((tiles, half, own_rows, COLUMN_TILE), bf16),
            pltpu.VMEM((tiles, half, own_rows, COLUMN_TILE), bf16),
            dma((7,)),
            dma,
            dma((heads,)),
            dma((ctx_size,)),
            dma((ctx_size,)),
            dma((heads,)),
            dma((ctx_size,)),
            dma((ctx_size,)),
            dma((head_size,)),
            dma((head_size,)),
            dma((tiles, half)),
            dma((tiles, half)),
            dma((tiles, half)),
            dma((tiles, half)),
        ],
        compiler_params=pltpu.CompilerParams(
            collective_id=0, has_side_effects=True, vmem_limit_bytes=56 * 1024 * 1024
        ),
    )(
        queries,
        keys,
        values,
        out_gate,
        log_decay.T,
        write_strength.T,
        segment_ids.reshape(1, rows),
        head_order,
        out_weight,
    )


def per_device(queries, keys, values, *rest):
    heads = values.shape[1] // DV
    one_owner_per_head = (
        heads == lax.axis_size("ctx")
        and queries.shape[0] == DK
        and lax.axis_size("head") % 2 == 0
    )
    form = head_owner if one_owner_per_head else gathered_prefix
    return form(queries, keys, values, *rest)


def solution(mesh):
    in_specs = (
        P("ctx", "head"),
        P("ctx", "head"),
        P("ctx", "head"),
        P("ctx", "head"),
        P("ctx", "head"),
        P("ctx", "head"),
        P("ctx"),
        P(),
        P("head", None),
    )
    out_specs = (P(("ctx", "head"), None), P("head", "ctx"))
    return jax.shard_map(
        per_device, mesh=mesh, in_specs=in_specs, out_specs=out_specs, check_vma=False
    )
```
